256 devices in a mesh: ctx: 32 (over y, z), ch: 8 (over x, core).
Axes of the slice: x: 4, y: 4, z: 8, core: 2. Of those that a mesh axis runs over, the one named last changes fastest.
Arguments:
- gate_in: bfloat16 [512, 131072], P('ch', 'ctx'), may hold values from -64 to 64
- key_in: bfloat16 [512, 131072], P('ch', 'ctx'), may hold values from -6 to 6
- value_in: bfloat16 [512, 131072], P('ch', 'ctx'), may hold values from -6 to 6
- long_filter: float32 [512, 131072], P('ch', 'ctx'), may hold values from -0.015625 to 0.015625
- skip_weight: float32 [512], P('ch'), may hold values from -1 to 1
- norm_gain: float32 [512], P('ch'), may hold values from 0.1 to 1.9
Outputs:
- mixed: bfloat16 [512, 131072], P('ch', 'ctx')
The draws below stay inside these ranges and needn't reach their ends.
All inputs are finite; a program needn't handle non-finite values.
Results may differ from the reference program's by a relative error of at most 0.001.
Values sent between devices are 32-bit elements; how exact they have to be, the bound alone decides.
A program may use at most 128 MiB of HBM per device.

```python
import jax
import jax.numpy as jnp
from jax import lax

CH = 512
LENGTH = 131072


def draw_gate_in(key, part):
    key = jax.random.fold_in(key, 7)
    first, second = jax.random.split(key)
    level = jnp.arange(CH, dtype=jnp.float32) / CH
    scale = 10.0 ** level * jnp.exp(jax.random.uniform(first, (CH,), minval=-0.2, maxval=0.2))
    values = jnp.clip(jax.random.normal(second, (CH, LENGTH)), -4.0, 4.0)
    return (values * scale[:, None]).astype(jnp.bfloat16)


def steps_of(rng, shape, cuts, low, top_value):
    def one(dim, parts):
        heights = jax.random.uniform(jax.random.fold_in(jax.random.fold_in(rng, 6), dim), (parts,), jnp.float32, low / len(cuts), top_value / len(cuts))
        return jnp.repeat(jnp.exp(heights), shape[dim] // parts).reshape((-1,) + (1,) * (len(shape) - dim - 1))

    loudness = one(*cuts[0])
    for cut in cuts[1:]:
        loudness = loudness * one(*cut)
    return loudness


def centred(stream_key, dims, scale, limit, cuts=(), kind=jnp.bfloat16):
    level = steps_of(stream_key, dims, cuts, -0.22, 0.18) if cuts else 1.0
    values = jax.random.normal(stream_key, dims, jnp.float32) * scale * level
    return jnp.minimum(jnp.maximum(values, -limit), limit).astype(kind)


def setup_inputs(seed: int = 0) -> dict:
    seeds = jax.random.split(jax.random.key(seed), 7)
    gate_in = draw_gate_in(jax.random.fold_in(seeds[6], 71), 0)
    key_in = centred(seeds[1], (CH, LENGTH), 1.0, 6.0, ((0, 8), (1, 32)))
    value_in = centred(seeds[2], (CH, LENGTH), 1.0, 6.0, ((0, 8), (1, 32)))
    long_filter = centred(seeds[3], (CH, LENGTH), LENGTH ** -0.5, 0.015625, ((0, 8), (1, 32)), jnp.float32)
    skip_weight = jnp.clip(jax.random.uniform(seeds[4], (CH,), jnp.float32, -1.0, 1.0) * steps_of(seeds[4], (CH,), ((0, 8),), -0.4, 0.0), -1.0, 1.0)
    norm_gain = jnp.clip(1.0 + 0.18 * jax.random.normal(seeds[5], (CH,), jnp.float32), 0.1, 1.9)
    return {"gate_in": gate_in, "key_in": key_in, "value_in": value_in, "long_filter": long_filter, "skip_weight": skip_weight, "norm_gain": norm_gain}


def reference(gate_in, key_in, value_in, long_filter, skip_weight, norm_gain):
    driven = key_in.astype(jnp.float32) * value_in.astype(jnp.float32)
    padded_len = 2 * LENGTH
    spec_driven = jnp.fft.rfft(driven, n=padded_len, axis=1)
    spec_filter = jnp.fft.rfft(long_filter, n=padded_len, axis=1)
    conv = jnp.fft.irfft(spec_driven * spec_filter, n=padded_len, axis=1)[:, :LENGTH]
    branch = gate_in.astype(jnp.float32) * (conv + skip_weight[:, None] * driven)
    power = lax.optimization_barrier(jnp.mean(branch * branch, axis=0))
    mixed = branch * norm_gain[:, None] * lax.rsqrt(power + 1e-06)[None, :]
    return mixed.astype(jnp.bfloat16)
```

```python
import jax
import jax.numpy as jnp
import numpy as np
from jax import lax
from jax.sharding import PartitionSpec as P

ROWS = 512
COLS = 256
SIZE = ROWS * COLS
SLOTS = 2
HIGH = lax.Precision.HIGH


def turn(num, den):
    angle = 2.0 * np.pi * ((num % den) / den)
    return np.cos(angle).astype(np.float32), (-np.sin(angle)).astype(np.float32)


def tables():
    freq = 4 * np.arange(ROWS, dtype=np.int64) + 1
    rows = np.arange(ROWS, dtype=np.int64)
    cols = np.arange(COLS, dtype=np.int64)
    first = turn(freq[:, None] * rows[None, :], 4 * ROWS)
    twiddle = turn(freq[:, None] * cols[None, :], 4 * SIZE)
    second = turn(cols[:, None] * cols[None, :], COLS)
    return first, twiddle, second


def body(gate_in, key_in, value_in, long_filter, skip_weight, norm_gain):
    channels, block = gate_in.shape
    blocks = lax.axis_size("ctx")
    (f_re, f_im), (t_re, t_im), (s_re, s_im) = tables()
    driven = key_in.astype(jnp.float32) * value_in.astype(jnp.float32)
    both = jnp.stack([driven, long_filter]).reshape(2, SLOTS, blocks, block // COLS, COLS)
    both = lax.all_to_all(both, "ctx", split_axis=2, concat_axis=2, tiled=True)
    both = both.reshape(2 * SLOTS, ROWS, COLS)
    first = np.concatenate([f_re, f_im])
    a = jnp.einsum("kr,brl->bkl", first, both, precision=HIGH)
    a_re, a_im = a[:, :ROWS], a[:, ROWS:]
    b = jnp.concatenate([a_re * t_re - a_im * t_im, a_re * t_im + a_im * t_re], axis=-1)
    second = np.block([[s_re, s_im], [-s_im, s_re]])
    spec = jnp.einsum("bkl,lm->bkm", b, second, precision=HIGH)
    x_re, x_im = spec[:SLOTS, :, :COLS], spec[:SLOTS, :, COLS:]
    h_re, h_im = spec[SLOTS:, :, :COLS], spec[SLOTS:, :, COLS:]
    prod = jnp.concatenate([x_re * h_re - x_im * h_im, x_re * h_im + x_im * h_re], axis=-1)
    back = np.block([[s_re, -s_im], [s_im, s_re]]) / np.float32(SIZE)
    c = jnp.einsum("bkm,ml->bkl", prod, back, precision=HIGH)
    c_re, c_im = c[..., :COLS], c[..., COLS:]
    d = jnp.concatenate([c_re * t_re + c_im * t_im, c_im * t_re - c_re * t_im], axis=1)
    last = np.concatenate([f_re, f_im]).T
    conv = jnp.einsum("rk,bkl->brl", last, d, precision=HIGH)
    conv = conv.reshape(SLOTS, blocks, block // COLS, COLS)
    conv = lax.all_to_all(conv, "ctx", split_axis=1, concat_axis=1, tiled=True)
    conv = conv.reshape(channels, block)
    branch = gate_in.astype(jnp.float32) * (conv + skip_weight[:, None] * driven)
    total = lax.psum(jnp.sum(branch * branch, axis=0), "ch")
    power = total / (channels * lax.axis_size("ch"))
    mixed = branch * norm_gain[:, None] * lax.rsqrt(power + 1e-6)[None, :]
    return mixed.astype(jnp.bfloat16)


def solution(mesh):
    specs = (P("ch", "ctx"), P("ch", "ctx"), P("ch", "ctx"), P("ch", "ctx"), P("ch"), P("ch"))
    return jax.shard_map(body, mesh=mesh, in_specs=specs, out_specs=P("ch", "ctx"), check_vma=False)
```

```python
import functools

import jax
import jax.numpy as jnp
import ml_dtypes
import numpy as np
from jax import lax
from jax.experimental import pallas as pl
from jax.experimental.pallas import tpu as pltpu
from jax.sharding import PartitionSpec as P

COLS = 256
SLOTS = 2
F32, BF16 = jnp.float32, jnp.bfloat16
DMA = pltpu.SemaphoreType.DMA


def turn(num, den):
    angle = 2.0 * np.pi * ((num % den) / den)
    return np.cos(angle), -np.sin(angle)


def halves(table):
    table = table.astype(np.float32)
    high = table.astype(ml_dtypes.bfloat16)
    low = (table - high.astype(np.float32)).astype(ml_dtypes.bfloat16)
    return high, low


def tables(rows, tile):
    size = rows * COLS
    freq = 4 * np.arange(rows, dtype=np.int64) + 1
    row, col = np.arange(rows, dtype=np.int64), np.arange(COLS, dtype=np.int64)
    f_re, f_im = turn(freq[:, None] * row[None, :], 4 * rows)
    t_re, t_im = turn(freq[:, None] * col[None, :], 4 * size)
    s_re, s_im = turn(col[:, None] * col[None, :], COLS)
    first = np.concatenate([f_re.reshape(-1, tile, rows), f_im.reshape(-1, tile, rows)], axis=1)
    second = np.block([[s_re, s_im], [-s_im, s_re]])
    back = np.block([[s_re, -s_im], [s_im, s_re]]) / size
    last = np.concatenate([f_re, f_im]).T
    twiddle = np.stack([t_re, t_im]).astype(np.float32)
    return (*halves(first), twiddle, *halves(second), *halves(back), *halves(last))


def split(value):
    high = value.astype(BF16)
    return high, (value - high.astype(F32)).astype(BF16)


def dot3(a_hi, a_lo, b_hi, b_lo):
    dot = functools.partial(jnp.dot, preferred_element_type=F32)
    return dot(a_hi, b_hi) + (dot(a_hi, b_lo) + dot(a_lo, b_hi))


def column(row):
    n = row.shape[1]
    eye = lax.broadcasted_iota(jnp.int32, (n, n), 0) == lax.broadcasted_iota(jnp.int32, (n, n), 1)
    return jnp.sum(jnp.where(eye, row, 0.0), axis=1, keepdims=True)


def kernel(
    n, groups, total_channels,
    gate_hbm, key_hbm, value_hbm, filter_hbm, skip_ref, gain_ref, *rest,
):
    tables_hbm, rest = rest[:9], rest[9:]
    out_ref, rest = rest[0], rest[1:]
    gate, key, value, filt = rest[:4]
    f_hi, f_lo, twiddle, s_hi, s_lo, b_hi, b_lo, l_hi, l_lo = tables_v = rest[4:13]
    (send_h, send_x, recv_h, recv_x, send_y, recv_y, x_hi, x_lo, mid_hi, mid_lo, spec_h, spec_x, d_hi, d_lo,
     branch, power, part, parts, in_sem, table_sem, out_sems, in_sems, ps_sem, pr_sem) = rest[13:]
    rows, wide = spec_h.shape
    tile = f_hi.shape[1] // 2
    channels, block = filt.shape
    ctx, ch = lax.axis_index("ctx"), lax.axis_index("ch")

    loads = [pltpu.make_async_copy(s, d, in_sem.at[i])
             for i, (s, d) in enumerate(((filter_hbm, filt), (key_hbm, key), (value_hbm, value), (gate_hbm, gate)))]
    for load in loads:
        load.start()
    table_loads = [pltpu.make_async_copy(s, d, table_sem.at[i]) for i, (s, d) in enumerate(zip(tables_hbm, tables_v))]
    for load in table_loads:
        load.start()

    barrier = pltpu.get_barrier_semaphore()

    def hello_ctx(i, _):
        pl.semaphore_signal(barrier, inc=1, device_id={"ctx": lax.rem(ctx + i, n)}, device_id_type=pl.DeviceIdType.MESH)
        return 0

    def hello_ch(i, _):
        pl.semaphore_signal(barrier, inc=1, device_id={"ch": lax.rem(ch + i, groups)},
                            device_id_type=pl.DeviceIdType.MESH)
        return 0

    lax.fori_loop(1, n, hello_ctx, 0)
    lax.fori_loop(1, groups, hello_ch, 0)

    def peer_of(i):
        if n % 8:
            return lax.rem(ctx + i, n)
        j = lax.rem(i, 8)
        odd = lax.rem(j, 2)
        step = odd * ((j + 1) // 2) + (1 - odd) * (8 - j // 2)
        fast = lax.rem(lax.rem(ctx, 8) + step, 8)
        slow = lax.rem(ctx // 8 + i // 8, n // 8)
        return slow * 8 + fast

    def exchange(src, dst, slot, kind):
        base = slot * n

        def one(i, _):
            p = peer_of(i)
            pltpu.make_async_remote_copy(
                src_ref=src.at[base + p], dst_ref=dst.at[base + ctx],
                send_sem=out_sems.at[kind, slot], recv_sem=in_sems.at[kind, slot],
                device_id={"ctx": p}, device_id_type=pl.DeviceIdType.MESH,
            ).start()
            return 0

        lax.fori_loop(1, n, one, 0)
        dst[pl.ds(base + ctx, 1)] = src[pl.ds(base + ctx, 1)]

    def arrived(dst, slot, kind):
        part = dst.at[pl.ds(0, n - 1)]
        pltpu.make_async_copy(part, part, in_sems.at[kind, slot]).wait()

    def lay_filter(slot, _):
        for c in range(0, n, 8):
            at = pl.ds(slot * n + c, 8)
            send_h[at] = filt[at].reshape(8, block // COLS, COLS)
        return 0

    def lay_driven(slot, _):
        for c in range(0, n, min(16, n)):
            at = pl.ds(slot * n + c, min(16, n))
            driven = key[at].astype(F32) * value[at].astype(F32)
            send_x[at] = driven.reshape(min(16, n), block // COLS, COLS)
        return 0

    def send_slot(slot, _):
        lay_filter(slot, 0)
        exchange(send_h, recv_h, slot, 0)
        lay_driven(slot, 0)
        exchange(send_x, recv_x, slot, 1)
        return 0

    for load in loads[:3]:
        load.wait()
    pl.semaphore_wait(barrier, (n - 1) + (groups - 1))
    lax.fori_loop(0, SLOTS, send_slot, 0)
    for load in table_loads:
        load.wait()

    def forward(src, slot, spec):
        x = src[pl.ds(slot * n, n)].reshape(rows, COLS)
        x_hi[...], x_lo[...] = split(x)

        def first(m, _):
            a = dot3(f_hi[m], f_lo[m], x_hi[...], x_lo[...])
            a_re, a_im = a[:tile], a[tile:]
            at = pl.ds(m * tile, tile)
            t_re, t_im = twiddle[0, at], twiddle[1, at]
            mid_hi[at, :COLS], mid_lo[at, :COLS] = split(a_re * t_re - a_im * t_im)
            mid_hi[at, COLS:], mid_lo[at, COLS:] = split(a_re * t_im + a_im * t_re)
            return 0

        def second(m, _):
            at = pl.ds(m * tile, tile)
            spec[at] = dot3(mid_hi[at], mid_lo[at], s_hi[...], s_lo[...])
            return 0

        lax.fori_loop(0, rows // tile, first, 0)
        lax.fori_loop(0, rows // tile, second, 0)

    def backward(slot):
        def first(m, _):
            at = pl.ds(m * tile, tile)
            x, h = spec_x[at], spec_h[at]
            x_re, x_im, h_re, h_im = x[:, :COLS], x[:, COLS:], h[:, :COLS], h[:, COLS:]
            p = jnp.concatenate([x_re * h_re - x_im * h_im, x_re * h_im + x_im * h_re], axis=1)
            c = dot3(*split(p), b_hi[...], b_lo[...])
            c_re, c_im = c[:, :COLS], c[:, COLS:]
            t_re, t_im = twiddle[0, at], twiddle[1, at]
            under = pl.ds(rows + m * tile, tile)
            d_hi[at], d_lo[at] = split(c_re * t_re + c_im * t_im)
            d_hi[under], d_lo[under] = split(c_im * t_re - c_re * t_im)
            return 0

        def second(m, _):
            at = pl.ds(m * tile, tile)
            y = dot3(l_hi[at], l_lo[at], d_hi[...], d_lo[...])
            blocks = tile // (block // COLS)
            send_y[pl.ds(slot * n + m * blocks, blocks)] = y.reshape(blocks, block // COLS, COLS)
            return 0

        lax.fori_loop(0, rows // tile, first, 0)
        lax.fori_loop(0, rows // tile, second, 0)

    def convolve(slot, _):
        arrived(recv_h, slot, 0)
        forward(recv_h, slot, spec_h)
        arrived(recv_x, slot, 1)
        forward(recv_x, slot, spec_x)
        backward(slot)
        exchange(send_y, recv_y, slot, 2)
        return 0

    lax.fori_loop(0, SLOTS, convolve, 0)
    loads[3].wait()
    skip, gain = column(skip_ref[...]), column(gain_ref[...])
    step = min(16, n)

    power[...] = jnp.zeros_like(power)
    for slot in range(SLOTS):
        arrived(recv_y, slot, 2)
        for c in range(slot * n, (slot + 1) * n, step):
            at = slice(c, c + step)
            driven = key[at].astype(F32) * value[at].astype(F32)
            conv = recv_y[at].reshape(step, block)
            b = gate[at].astype(F32) * (conv + skip[at] * driven)
            branch[at] = b
            square = b * b
            power[...] += sum(square[r:r + 8] for r in range(0, step, 8))
    part[...] = jnp.sum(power[...], axis=0, keepdims=True)

    def share(i, _):
        pltpu.make_async_remote_copy(
            src_ref=part, dst_ref=parts.at[ch], send_sem=ps_sem, recv_sem=pr_sem,
            device_id={"ch": lax.rem(ch + i, groups)}, device_id_type=pl.DeviceIdType.MESH,
        ).start()
        return 0

    lax.fori_loop(1, groups, share, 0)
    parts[pl.ds(ch, 1)] = part[...].reshape(1, 1, block)
    others = parts.at[pl.ds(0, groups - 1)]
    pltpu.make_async_copy(others, others, pr_sem).wait()
    mean = jnp.sum(parts[...], axis=0) / total_channels
    norm = lax.rsqrt(mean + 1e-6)
    for c in range(0, channels, step):
        at = slice(c, c + step)
        out_ref[at] = (branch[at] * gain[at] * norm).astype(BF16)

    pltpu.make_async_copy(others, others, ps_sem).wait()
    for kind, src in enumerate((send_h, send_x, send_y)):
        for slot in range(SLOTS):
            sent = src.at[pl.ds(0, n - 1)]
            pltpu.make_async_copy(sent, sent, out_sems.at[kind, slot]).wait()


def solution(mesh):
    n, groups = mesh.shape["ctx"], mesh.shape["ch"]

    def body(gate_in, key_in, value_in, long_filter, skip_weight, norm_gain):
        channels, block = gate_in.shape
        rows = n * block // COLS
        tile = min(128, rows)
        blocks = pltpu.VMEM((channels, block // COLS, COLS), F32)
        constants = tables(rows, tile)
        vmem, anywhere = pl.BlockSpec(memory_space=pltpu.VMEM), pl.BlockSpec(memory_space=pl.ANY)
        return pl.pallas_call(
            functools.partial(kernel, n, groups, channels * groups),
            out_shape=jax.ShapeDtypeStruct((channels, block), BF16),
            in_specs=[anywhere] * 4 + [vmem] * 2 + [anywhere] * len(constants),
            out_specs=vmem,
            scratch_shapes=[
                pltpu.VMEM((channels, block), BF16),
                pltpu.VMEM((channels, block), BF16),
                pltpu.VMEM((channels, block), BF16),
                pltpu.VMEM((channels, block), F32),
                *[pltpu.VMEM(c.shape, c.dtype) for c in constants],
                blocks, blocks, blocks, blocks, blocks, blocks,
                pltpu.VMEM((rows, COLS), BF16), pltpu.VMEM((rows, COLS), BF16),
                pltpu.VMEM((rows, 2 * COLS), BF16), pltpu.VMEM((rows, 2 * COLS), BF16),
                pltpu.VMEM((rows, 2 * COLS), F32), pltpu.VMEM((rows, 2 * COLS), F32),
                pltpu.VMEM((2 * rows, COLS), BF16), pltpu.VMEM((2 * rows, COLS), BF16),
                pltpu.VMEM((channels, block), F32),
                pltpu.VMEM((8, block), F32),
                pltpu.VMEM((1, block), F32),
                pltpu.VMEM((groups, 1, block), F32),
                DMA((4,)), DMA((len(constants),)),
                DMA((3, SLOTS)), DMA((3, SLOTS)), DMA, DMA,
            ],
            compiler_params=pltpu.CompilerParams(
                collective_id=0, has_side_effects=True, vmem_limit_bytes=50 * 1024 * 1024),
            cost_estimate=pl.CostEstimate(flops=10**10, bytes_accessed=12 * 2**20, transcendentals=4096),
        )(gate_in, key_in, value_in, long_filter, skip_weight.reshape(1, channels), norm_gain.reshape(1, channels),
          *[jnp.asarray(c) for c in constants])

    specs = (P("ch", "ctx"), P("ch", "ctx"), P("ch", "ctx"), P("ch", "ctx"), P("ch"), P("ch"))
    return jax.shard_map(body, mesh=mesh, in_specs=specs, out_specs=P("ch", "ctx"), check_vma=False)
```

```python
import functools

import jax
import jax.numpy as jnp
import ml_dtypes
import numpy as np
from jax import lax
from jax.experimental import pallas as pl
from jax.experimental.pallas import tpu as pltpu
from jax.sharding import PartitionSpec as P

COLS = 256
SLOTS = 2
F32, BF16 = jnp.float32, jnp.bfloat16
VMEM_LIMIT = 63 * 2**20
DMA = pltpu.SemaphoreType.DMA


def turn(num, den):
    angle = 2.0 * np.pi * ((num % den) / den)
    return np.cos(angle), -np.sin(angle)


def halves(table):
    table = table.astype(np.float32)
    high = table.astype(ml_dtypes.bfloat16)
    low = (table - high.astype(np.float32)).astype(ml_dtypes.bfloat16)
    return high, low


def tables(rows, tile):
    size = rows * COLS
    freq = 4 * np.arange(rows, dtype=np.int64) + 1
    row, col = np.arange(rows, dtype=np.int64), np.arange(COLS, dtype=np.int64)
    f_re, f_im = turn(freq[:, None] * row[None, :], 4 * rows)
    t_re, t_im = turn(freq[:, None] * col[None, :], 4 * size)
    s_re, s_im = turn(col[:, None] * col[None, :], COLS)
    first = np.concatenate([f_re.reshape(-1, tile, rows), f_im.reshape(-1, tile, rows)], axis=1).reshape(2 * rows, rows)
    second = np.block([[s_re, s_im], [-s_im, s_re]])
    back = np.block([[s_re, -s_im], [s_im, s_re]]) / size
    last = np.concatenate([f_re.T, f_im.T])
    twiddle = np.stack([t_re, t_im]).astype(np.float32)
    wide = max(rows, 2 * COLS)
    stacked = np.concatenate([np.pad(t, ((0, 0), (0, wide - t.shape[1]))) for t in (first, last, second, back)])
    return np.stack(halves(stacked)), twiddle


def split(value):
    high = value.astype(BF16)
    return high, (value - high.astype(F32)).astype(BF16)


def dot3(a_hi, a_lo, b_hi, b_lo):
    dot = functools.partial(jnp.dot, preferred_element_type=F32)
    return dot(a_hi, b_hi) + (dot(a_hi, b_lo) + dot(a_lo, b_hi))


def column(row):
    n = row.shape[1]
    eye = lax.broadcasted_iota(jnp.int32, (n, n), 0) == lax.broadcasted_iota(jnp.int32, (n, n), 1)
    return jnp.sum(jnp.where(eye, row, 0.0), axis=1, keepdims=True)


def kernel(
    n, groups, total_channels,
    gate_hbm, key_hbm, value_hbm, filter_hbm, skip_hbm, gain_hbm, *rest,
):
    tables_hbm, (out_hbm, *rest) = rest[:2], rest[2:]
    gate, key, value, filt, skip_ref, gain_ref = rest[:6]
    matrices, twiddle = tables_v = rest[6:8]
    (send_h, send_x, recv_h, recv_x, send_y, recv_y, x_hi, x_lo, mid_hi, mid_lo, spec_h, spec_x, d_hi, d_lo,
     gated, direct, scaled, power, part, parts, mixed,
     load_sems, table_sem, out_sems, in_sems, back_sems, ps_sem, pr_sem, store_sem) = rest[8:]
    rows, wide = spec_h.shape
    tile = min(128, rows)
    f_at, l_at, s_at, b_at = 0, 2 * rows, 4 * rows, 4 * rows + wide
    channels, block = gate.shape
    ctx, ch = lax.axis_index("ctx"), lax.axis_index("ch")
    step = min(16, n)
    ring = min(8, n)
    mesh_id = pl.DeviceIdType.MESH

    def half(ref, slot):
        return ref.at[pl.ds(slot * n, n)]

    pairs = [(half(filter_hbm, 0), half(filt, 0)), (key_hbm, key), (value_hbm, value), (half(filter_hbm, 1), half(filt, 1)),
             (gate_hbm, gate), (skip_hbm, skip_ref), (gain_hbm, gain_ref)]
    loads = [pltpu.make_async_copy(s, d, load_sems.at[i]) for i, (s, d) in enumerate(pairs)]
    table_loads = [pltpu.make_async_copy(s, d, table_sem.at[i]) for i, (s, d) in enumerate(zip(tables_hbm, tables_v))]
    for load in loads + table_loads:
        load.start()

    barrier = pltpu.get_barrier_semaphore()

    def hello_ctx(i, _):
        pl.semaphore_signal(barrier, inc=1, device_id={"ctx": lax.rem(ctx + i, n)}, device_id_type=mesh_id)
        return 0

    def hello_ch(i, _):
        pl.semaphore_signal(barrier, inc=1, device_id={"ch": lax.rem(ch + i, groups)}, device_id_type=mesh_id)
        return 0

    lax.fori_loop(1, n, hello_ctx, 0)
    lax.fori_loop(1, groups, hello_ch, 0)

    def peer_of(i):
        j = lax.rem(i, ring)
        odd = lax.rem(j, 2)
        move = odd * ((j + 1) // 2) + (1 - odd) * (ring - j // 2)
        fast = lax.rem(lax.rem(ctx, ring) + move, ring)
        slow = lax.rem(ctx // ring + i // ring, n // ring)
        return slow * ring + fast

    def exchange(src, dst, slot, kind):
        base = slot * n

        def one(i, _):
            p = peer_of(i)
            arrival = back_sems.at[slot, i // ring] if kind == 2 else in_sems.at[kind, slot]
            pltpu.make_async_remote_copy(
                src_ref=src.at[base + p], dst_ref=dst.at[base + ctx], send_sem=out_sems.at[kind],
                recv_sem=arrival, device_id={"ctx": p}, device_id_type=mesh_id,
            ).start()
            return 0

        lax.fori_loop(1, n, one, 0)
        dst[pl.ds(base + ctx, 1)] = src[pl.ds(base + ctx, 1)]

    def landed(dst, count, sem):
        some = dst.at[pl.ds(0, count)]
        pltpu.make_async_copy(some, some, sem).wait()

    def lay_filter(slot):
        for c in range(0, n, 8):
            at = pl.ds(slot * n + c, 8)
            send_h[at] = filt[at].reshape(8, block // COLS, COLS)

    def lay_driven(slot):
        for c in range(0, n, step):
            at = pl.ds(slot * n + c, step)
            driven = key[at].astype(F32) * value[at].astype(F32)
            send_x[at] = driven.reshape(step, block // COLS, COLS)

    for load in loads[:4]:
        load.wait()
    pl.semaphore_wait(barrier, (n - 1) + (groups - 1))
    for slot in range(SLOTS):
        lay_filter(slot)
        exchange(send_h, recv_h, slot, 0)
        lay_driven(slot)
        exchange(send_x, recv_x, slot, 1)
    for load in loads[4:]:
        load.wait()

    skip, gain = column(skip_ref[...]), column(gain_ref[...])
    for c in range(0, channels, step):
        at = slice(c, c + step)
        gated[at] = gate[at].astype(F32)
        direct[at] = skip[at] * (key[at].astype(F32) * value[at].astype(F32))
    for load in table_loads:
        load.wait()

    def matrix(start, count, width):
        at = pl.ds(start, count)
        return matrices[0, at, :width], matrices[1, at, :width]

    def forward(src, slot, spec):
        x = src[pl.ds(slot * n, n)].reshape(rows, COLS)
        x_hi[...], x_lo[...] = split(x)

        def first(m, _):
            a = dot3(*matrix(f_at + m * 2 * tile, 2 * tile, rows), x_hi[...], x_lo[...])
            a_re, a_im = a[:tile], a[tile:]
            at = pl.ds(m * tile, tile)
            t_re, t_im = twiddle[0, at], twiddle[1, at]
            mid_hi[at, :COLS], mid_lo[at, :COLS] = split(a_re * t_re - a_im * t_im)
            mid_hi[at, COLS:], mid_lo[at, COLS:] = split(a_re * t_im + a_im * t_re)
            return 0

        def second(m, _):
            at = pl.ds(m * tile, tile)
            spec[at] = dot3(mid_hi[at], mid_lo[at], *matrix(s_at, wide, wide))
            return 0

        lax.fori_loop(0, rows // tile, first, 0)
        lax.fori_loop(0, rows // tile, second, 0)

    def backward(slot):
        def first(m, _):
            at = pl.ds(m * tile, tile)
            x, h = spec_x[at], spec_h[at]
            x_re, x_im, h_re, h_im = x[:, :COLS], x[:, COLS:], h[:, :COLS], h[:, COLS:]
            p = jnp.concatenate([x_re * h_re - x_im * h_im, x_re * h_im + x_im * h_re], axis=1)
            c = dot3(*split(p), *matrix(b_at, wide, wide))
            c_re, c_im = c[:, :COLS], c[:, COLS:]
            t_re, t_im = twiddle[0, at], twiddle[1, at]
            under = pl.ds(rows + m * tile, tile)
            d_hi[at], d_lo[at] = split(c_re * t_re + c_im * t_im)
            d_hi[under], d_lo[under] = split(c_im * t_re - c_re * t_im)
            return 0

        def second(m, _):
            at = pl.ds(m * tile, tile)
            y = dot3(*matrix(l_at + m * tile, tile, rows), d_hi[:rows], d_lo[:rows])
            y += dot3(*matrix(l_at + rows + m * tile, tile, rows), d_hi[rows:], d_lo[rows:])
            blocks = tile // (block // COLS)
            send_y[pl.ds(slot * n + m * blocks, blocks)] = y.reshape(blocks, block // COLS, COLS)
            return 0

        lax.fori_loop(0, rows // tile, first, 0)
        lax.fori_loop(0, rows // tile, second, 0)

    def convolve(slot, _):
        landed(recv_h, n - 1, in_sems.at[0, slot])
        forward(recv_h, slot, spec_h)
        landed(recv_x, n - 1, in_sems.at[1, slot])
        forward(recv_x, slot, spec_x)
        backward(slot)
        exchange(send_y, recv_y, slot, 2)
        return 0

    lax.fori_loop(0, SLOTS, convolve, 0)

    power[...] = jnp.zeros_like(power)
    for slot in range(SLOTS):
        for away in range(n // ring):
            landed(recv_y, ring - (away == 0), back_sems.at[slot, away])
            owner = lax.rem(ctx // ring + (n // ring - away), n // ring)
            at = pl.ds(pl.multiple_of(slot * n + owner * ring, ring), ring)
            conv = recv_y[at].reshape(ring, block)
            branch = gated[at] * (conv + direct[at])
            scaled[at] = branch
            power[...] += branch * branch
    part[...] = jnp.sum(power[...], axis=0, keepdims=True)

    def share(i, _):
        pltpu.make_async_remote_copy(
            src_ref=part, dst_ref=parts.at[ch], send_sem=ps_sem, recv_sem=pr_sem,
            device_id={"ch": lax.rem(ch + i, groups)}, device_id_type=mesh_id,
        ).start()
        return 0

    lax.fori_loop(1, groups, share, 0)
    parts[pl.ds(ch, 1)] = part[...].reshape(1, 1, block)
    landed(parts, groups - 1, pr_sem)
    mean = jnp.sum(parts[...], axis=0) / total_channels
    norm = lax.rsqrt(mean + 1e-6)
    for c in range(0, channels, step):
        at = slice(c, c + step)
        mixed[at] = (scaled[at] * gain[at] * norm).astype(BF16)
        pltpu.make_async_copy(mixed.at[at], out_hbm.at[at], store_sem).start()

    landed(parts, groups - 1, ps_sem)
    for kind, src in enumerate((send_h, send_x, send_y)):
        landed(src, SLOTS * (n - 1), out_sems.at[kind])
    pltpu.make_async_copy(mixed, out_hbm, store_sem).wait()


def solution(mesh):
    n, groups = mesh.shape["ctx"], mesh.shape["ch"]

    def body(gate_in, key_in, value_in, long_filter, skip_weight, norm_gain):
        channels, block = gate_in.shape
        rows = n * block // COLS
        tile = min(128, rows)
        blocks = pltpu.VMEM((channels, block // COLS, COLS), F32)
        half, full = pltpu.VMEM((channels, block), BF16), pltpu.VMEM((channels, block), F32)
        constants = tables(rows, tile)
        hbm = pl.BlockSpec(memory_space=pltpu.HBM)
        return pl.pallas_call(
            functools.partial(kernel, n, groups, channels * groups),
            out_shape=jax.ShapeDtypeStruct((channels, block), BF16),
            in_specs=[hbm] * (6 + len(constants)),
            out_specs=hbm,
            scratch_shapes=[
                half, half, half, full,
                pltpu.VMEM((1, channels), F32), pltpu.VMEM((1, channels), F32),
                *[pltpu.VMEM(c.shape, c.dtype) for c in constants],
                blocks, blocks, blocks, blocks, blocks, blocks,
                pltpu.VMEM((rows, COLS), BF16), pltpu.VMEM((rows, COLS), BF16),
                pltpu.VMEM((rows, 2 * COLS), BF16), pltpu.VMEM((rows, 2 * COLS), BF16),
                pltpu.VMEM((rows, 2 * COLS), F32), pltpu.VMEM((rows, 2 * COLS), F32),
                pltpu.VMEM((2 * rows, COLS), BF16), pltpu.VMEM((2 * rows, COLS), BF16),
                full, full, full,
                pltpu.VMEM((min(8, n), block), F32),
                pltpu.VMEM((1, block), F32),
                pltpu.VMEM((groups, 1, block), F32),
                half,
                DMA((7,)), DMA((len(constants),)), DMA((3,)), DMA((2, SLOTS)), DMA((SLOTS, n // min(8, n))),
                DMA, DMA, DMA,
            ],
            compiler_params=pltpu.CompilerParams(
                collective_id=0, has_side_effects=True, vmem_limit_bytes=VMEM_LIMIT),
            cost_estimate=pl.CostEstimate(flops=10**10, bytes_accessed=12 * 2**20, transcendentals=4096),
        )(gate_in, key_in, value_in, long_filter, skip_weight.reshape(1, channels), norm_gain.reshape(1, channels),
          *[jnp.asarray(c) for c in constants])

    specs = (P("ch", "ctx"), P("ch", "ctx"), P("ch", "ctx"), P("ch", "ctx"), P("ch"), P("ch"))
    return jax.shard_map(body, mesh=mesh, in_specs=specs, out_specs=P("ch", "ctx"), check_vma=False)
```

```python
import functools

import jax
import jax.numpy as jnp
import ml_dtypes
import numpy as np
from jax import lax
from jax.experimental import pallas as pl
from jax.experimental.pallas import tpu as pltpu
from jax.sharding import PartitionSpec as P

COLS = 256
SLOTS = 2
F32, BF16 = jnp.float32, jnp.bfloat16
VMEM_LIMIT = 63 * 2**20
EARLY = (0, 24, 8, 16, 25, 1, 9, 17, 26, 2, 10, 18, 27, 3, 11, 19)
DMA = pltpu.SemaphoreType.DMA


def turn(num, den):
    angle = 2.0 * np.pi * ((num % den) / den)
    return np.cos(angle), -np.sin(angle)


def halves(table):
    table = table.astype(np.float32)
    high = table.astype(ml_dtypes.bfloat16)
    low = (table - high.astype(np.float32)).astype(ml_dtypes.bfloat16)
    return high, low


def tables(rows, tile):
    size = rows * COLS
    freq = 4 * np.arange(rows, dtype=np.int64) + 1
    row, col = np.arange(rows, dtype=np.int64), np.arange(COLS, dtype=np.int64)
    f_re, f_im = turn(freq[:, None] * row[None, :], 4 * rows)
    t_re, t_im = turn(freq[:, None] * col[None, :], 4 * size)
    s_re, s_im = turn(col[:, None] * col[None, :], COLS)
    first = np.concatenate([f_re.reshape(-1, tile, rows), f_im.reshape(-1, tile, rows)], axis=1).reshape(2 * rows, rows)
    second = np.block([[s_re, s_im], [-s_im, s_re]])
    back = np.block([[s_re, -s_im], [s_im, s_re]]) / size
    last = np.concatenate([f_re.T, f_im.T])
    twiddle = np.stack([t_re, t_im]).astype(np.float32)
    wide = max(rows, 2 * COLS)
    stacked = np.concatenate([np.pad(t, ((0, 0), (0, wide - t.shape[1]))) for t in (first, last, second, back)])
    return np.stack(halves(stacked)), twiddle


def split(value):
    high = value.astype(BF16)
    return high, (value - high.astype(F32)).astype(BF16)


def dot3(a_hi, a_lo, b_hi, b_lo):
    dot = functools.partial(jnp.dot, preferred_element_type=F32)
    return dot(a_hi, b_hi) + (dot(a_hi, b_lo) + dot(a_lo, b_hi))


def column(row):
    n = row.shape[1]
    eye = lax.broadcasted_iota(jnp.int32, (n, n), 0) == lax.broadcasted_iota(jnp.int32, (n, n), 1)
    return jnp.sum(jnp.where(eye, row, 0.0), axis=1, keepdims=True)


def kernel(
    n, groups, total_channels,
    gate_hbm, key_hbm, value_hbm, filter_hbm, skip_hbm, gain_hbm, *rest,
):
    tables_hbm, (out_hbm, *rest) = rest[:2], rest[2:]
    gate, key, value, filt, skip_ref, gain_ref = rest[:6]
    matrices, twiddle = tables_v = rest[6:8]
    (send_h, send_x, recv_h, recv_x, send_y, recv_y, x_hi, x_lo, mid_hi, mid_lo, spec_h, spec_x, d_hi, d_lo,
     gated, direct, scaled, power, part, parts, mixed,
     load_sems, table_sem, out_sems, in_sems, back_sems, ps_sem, pr_sem, store_sem) = rest[8:]
    rows, wide = spec_h.shape
    tile = min(128, rows)
    f_at, l_at, s_at, b_at = 0, 2 * rows, 4 * rows, 4 * rows + wide
    channels, block = gate.shape
    ctx, ch = lax.axis_index("ctx"), lax.axis_index("ch")
    step = min(16, n)
    ring = min(8, n)
    mesh_id = pl.DeviceIdType.MESH

    def half(ref, slot):
        return ref.at[pl.ds(slot * n, n)]

    pairs = [(half(filter_hbm, 0), half(filt, 0)), (key_hbm, key), (value_hbm, value), (half(filter_hbm, 1), half(filt, 1)),
             (gate_hbm, gate), (skip_hbm, skip_ref), (gain_hbm, gain_ref)]
    loads = [pltpu.make_async_copy(s, d, load_sems.at[i]) for i, (s, d) in enumerate(pairs)]
    table_loads = [pltpu.make_async_copy(s, d, table_sem.at[i]) for i, (s, d) in enumerate(zip(tables_hbm, tables_v))]
    for load in loads[:4]:
        load.start()

    barrier = pltpu.get_barrier_semaphore()

    def hello_ctx(i, _):
        pl.semaphore_signal(barrier, inc=1, device_id={"ctx": lax.rem(ctx + i, n)}, device_id_type=mesh_id)
        return 0

    def hello_ch(i, _):
        pl.semaphore_signal(barrier, inc=1, device_id={"ch": lax.rem(ch + i, groups)}, device_id_type=mesh_id)
        return 0

    lax.fori_loop(1, n, hello_ctx, 0)
    lax.fori_loop(1, groups, hello_ch, 0)

    def peer_of(i):
        j = lax.rem(i, ring)
        odd = lax.rem(j, 2)
        move = odd * ((j + 1) // 2) + (1 - odd) * (ring - j // 2)
        fast = lax.rem(lax.rem(ctx, ring) + move, ring)
        slow = lax.rem(ctx // ring + i // ring, n // ring)
        return slow * ring + fast

    def exchange(src, dst, slot, kind, first=()):
        base = slot * n

        def push(p, group):
            arrival = back_sems.at[slot, group] if kind == 2 else in_sems.at[kind, slot]
            pltpu.make_async_remote_copy(
                src_ref=src.at[base + p], dst_ref=dst.at[base + ctx], send_sem=out_sems.at[kind],
                recv_sem=arrival, device_id={"ctx": p}, device_id_type=mesh_id,
            ).start()

        def one(i, _):
            p = peer_of(i)
            if first:
                later = functools.reduce(jnp.logical_and, [p != q for q in first])
                pl.when(later)(lambda: push(p, i // ring))
            else:
                push(p, i // ring)
            return 0

        for q in first:
            group = lax.rem(q // ring + n // ring - ctx // ring, n // ring)
            pl.when(ctx != q)(lambda q=q, group=group: push(q, group))
        lax.fori_loop(1, n, one, 0)
        dst[pl.ds(base + ctx, 1)] = src[pl.ds(base + ctx, 1)]

    def landed(dst, count, sem):
        some = dst.at[pl.ds(0, count)]
        pltpu.make_async_copy(some, some, sem).wait()

    def lay_filter(slot):
        for c in range(0, n, 8):
            at = pl.ds(slot * n + c, 8)
            send_h[at] = filt[at].reshape(8, block // COLS, COLS)

    def lay_driven(slot):
        for c in range(0, n, step):
            at = pl.ds(slot * n + c, step)
            driven = key[at].astype(F32) * value[at].astype(F32)
            send_x[at] = driven.reshape(step, block // COLS, COLS)

    loads[0].wait()
    pl.semaphore_wait(barrier, (n - 1) + (groups - 1))
    lay_filter(0)
    exchange(send_h, recv_h, 0, 0)
    loads[1].wait()
    loads[2].wait()
    lay_driven(0)
    exchange(send_x, recv_x, 0, 1)
    loads[3].wait()
    lay_filter(1)
    exchange(send_h, recv_h, 1, 0)
    lay_driven(1)
    exchange(send_x, recv_x, 1, 1)
    for load in loads[4:] + table_loads:
        load.start()
    for load in loads[4:]:
        load.wait()

    skip, gain = column(skip_ref[...]), column(gain_ref[...])
    for c in range(0, channels, step):
        at = slice(c, c + step)
        gated[at] = gate[at].astype(F32)
        direct[at] = skip[at] * (key[at].astype(F32) * value[at].astype(F32))
    for load in table_loads:
        load.wait()

    def matrix(start, count, width):
        at = pl.ds(start, count)
        return matrices[0, at, :width], matrices[1, at, :width]

    def forward(src, slot, spec):
        x = src[pl.ds(slot * n, n)].reshape(rows, COLS)
        x_hi[...], x_lo[...] = split(x)

        def first(m, _):
            a = dot3(*matrix(f_at + m * 2 * tile, 2 * tile, rows), x_hi[...], x_lo[...])
            a_re, a_im = a[:tile], a[tile:]
            at = pl.ds(m * tile, tile)
            t_re, t_im = twiddle[0, at], twiddle[1, at]
            mid_hi[at, :COLS], mid_lo[at, :COLS] = split(a_re * t_re - a_im * t_im)
            mid_hi[at, COLS:], mid_lo[at, COLS:] = split(a_re * t_im + a_im * t_re)
            return 0

        def second(m, _):
            at = pl.ds(m * tile, tile)
            spec[at] = dot3(mid_hi[at], mid_lo[at], *matrix(s_at, wide, wide))
            return 0

        lax.fori_loop(0, rows // tile, first, 0)
        lax.fori_loop(0, rows // tile, second, 0)

    def backward(slot):
        def first(m, _):
            at = pl.ds(m * tile, tile)
            x, h = spec_x[at], spec_h[at]
            x_re, x_im, h_re, h_im = x[:, :COLS], x[:, COLS:], h[:, :COLS], h[:, COLS:]
            p = jnp.concatenate([x_re * h_re - x_im * h_im, x_re * h_im + x_im * h_re], axis=1)
            c = dot3(*split(p), *matrix(b_at, wide, wide))
            c_re, c_im = c[:, :COLS], c[:, COLS:]
            t_re, t_im = twiddle[0, at], twiddle[1, at]
            under = pl.ds(rows + m * tile, tile)
            d_hi[at], d_lo[at] = split(c_re * t_re + c_im * t_im)
            d_hi[under], d_lo[under] = split(c_im * t_re - c_re * t_im)
            return 0

        def second(m, _):
            at = pl.ds(m * tile, tile)
            y = dot3(*matrix(l_at + m * tile, tile, rows), d_hi[:rows], d_lo[:rows])
            y += dot3(*matrix(l_at + rows + m * tile, tile, rows), d_hi[rows:], d_lo[rows:])
            blocks = tile // (block // COLS)
            send_y[pl.ds(slot * n + m * blocks, blocks)] = y.reshape(blocks, block // COLS, COLS)
            return 0

        lax.fori_loop(0, rows // tile, first, 0)
        lax.fori_loop(0, rows // tile, second, 0)

    def convolve(slot):
        landed(recv_h, n - 1, in_sems.at[0, slot])
        forward(recv_h, slot, spec_h)
        landed(recv_x, n - 1, in_sems.at[1, slot])
        forward(recv_x, slot, spec_x)
        backward(slot)

    early = tuple(q for q in EARLY if q < n)
    for slot in range(SLOTS):
        convolve(slot)
        exchange(send_y, recv_y, slot, 2, early if slot == SLOTS - 1 else ())

    power[...] = jnp.zeros_like(power)
    for slot in range(SLOTS):
        for away in range(n // ring):
            landed(recv_y, ring - (away == 0), back_sems.at[slot, away])
            owner = lax.rem(ctx // ring + (n // ring - away), n // ring)
            at = pl.ds(pl.multiple_of(slot * n + owner * ring, ring), ring)
            conv = recv_y[at].reshape(ring, block)
            branch = gated[at] * (conv + direct[at])
            scaled[at] = branch
            power[...] += branch * branch
    part[...] = jnp.sum(power[...], axis=0, keepdims=True)

    def share(i, _):
        pltpu.make_async_remote_copy(
            src_ref=part, dst_ref=parts.at[ch], send_sem=ps_sem, recv_sem=pr_sem,
            device_id={"ch": lax.rem(ch + i, groups)}, device_id_type=mesh_id,
        ).start()
        return 0

    lax.fori_loop(1, groups, share, 0)
    parts[pl.ds(ch, 1)] = part[...].reshape(1, 1, block)
    landed(parts, groups - 1, pr_sem)
    mean = jnp.sum(parts[...], axis=0) / total_channels
    norm = lax.rsqrt(mean + 1e-6)
    for c in range(0, channels, step):
        at = slice(c, c + step)
        mixed[at] = (scaled[at] * gain[at] * norm).astype(BF16)
        pltpu.make_async_copy(mixed.at[at], out_hbm.at[at], store_sem).start()

    landed(parts, groups - 1, ps_sem)
    for kind, src in enumerate((send_h, send_x, send_y)):
        landed(src, SLOTS * (n - 1), out_sems.at[kind])
    pltpu.make_async_copy(mixed, out_hbm, store_sem).wait()


def solution(mesh):
    n, groups = mesh.shape["ctx"], mesh.shape["ch"]

    def body(gate_in, key_in, value_in, long_filter, skip_weight, norm_gain):
        channels, block = gate_in.shape
        rows = n * block // COLS
        tile = min(128, rows)
        blocks = pltpu.VMEM((channels, block // COLS, COLS), F32)
        half, full = pltpu.VMEM((channels, block), BF16), pltpu.VMEM((channels, block), F32)
        constants = tables(rows, tile)
        hbm = pl.BlockSpec(memory_space=pltpu.HBM)
        return pl.pallas_call(
            functools.partial(kernel, n, groups, channels * groups),
            out_shape=jax.ShapeDtypeStruct((channels, block), BF16),
            in_specs=[hbm] * (6 + len(constants)),
            out_specs=hbm,
            scratch_shapes=[
                half, half, half, full,
                pltpu.VMEM((1, channels), F32), pltpu.VMEM((1, channels), F32),
                *[pltpu.VMEM(c.shape, c.dtype) for c in constants],
                blocks, blocks, blocks, blocks, blocks, blocks,
                pltpu.VMEM((rows, COLS), BF16), pltpu.VMEM((rows, COLS), BF16),
                pltpu.VMEM((rows, 2 * COLS), BF16), pltpu.VMEM((rows, 2 * COLS), BF16),
                pltpu.VMEM((rows, 2 * COLS), F32), pltpu.VMEM((rows, 2 * COLS), F32),
                pltpu.VMEM((2 * rows, COLS), BF16), pltpu.VMEM((2 * rows, COLS), BF16),
                full, full, full,
                pltpu.VMEM((min(8, n), block), F32),
                pltpu.VMEM((1, block), F32),
                pltpu.VMEM((groups, 1, block), F32),
                half,
                DMA((7,)), DMA((len(constants),)), DMA((3,)), DMA((2, SLOTS)), DMA((SLOTS, n // min(8, n))),
                DMA, DMA, DMA,
            ],
            compiler_params=pltpu.CompilerParams(
                collective_id=0, has_side_effects=True, vmem_limit_bytes=VMEM_LIMIT),
            cost_estimate=pl.CostEstimate(flops=10**10, bytes_accessed=12 * 2**20, transcendentals=4096),
        )(gate_in, key_in, value_in, long_filter, skip_weight.reshape(1, channels), norm_gain.reshape(1, channels),
          *[jnp.asarray(c) for c in constants])

    specs = (P("ch", "ctx"), P("ch", "ctx"), P("ch", "ctx"), P("ch", "ctx"), P("ch"), P("ch"))
    return jax.shard_map(body, mesh=mesh, in_specs=specs, out_specs=P("ch", "ctx"), check_vma=False)
```

```python
import functools

import jax
import jax.numpy as jnp
import ml_dtypes
import numpy as np
from jax import lax
from jax.experimental import pallas as pl
from jax.experimental.pallas import tpu as pltpu
from jax.sharding import PartitionSpec as P

COLS = 256
SLOTS = 2
F32, BF16 = jnp.float32, jnp.bfloat16
VMEM_LIMIT = 63 * 2**20
EARLY = (0, 24, 8, 1, 16, 25, 9, 2, 17, 10, 26, 18, 3, 11, 27, 19)
DMA = pltpu.SemaphoreType.DMA


def turn(num, den):
    angle = 2.0 * np.pi * ((num % den) / den)
    return np.cos(angle), -np.sin(angle)


def halves(table):
    table = table.astype(np.float32)
    high = table.astype(ml_dtypes.bfloat16)
    low = (table - high.astype(np.float32)).astype(ml_dtypes.bfloat16)
    return high, low


def tables(rows, tile):
    size = rows * COLS
    freq = 4 * np.arange(rows, dtype=np.int64) + 1
    row, col = np.arange(rows, dtype=np.int64), np.arange(COLS, dtype=np.int64)
    f_re, f_im = turn(freq[:, None] * row[None, :], 4 * rows)
    t_re, t_im = turn(freq[:, None] * col[None, :], 4 * size)
    s_re, s_im = turn(col[:, None] * col[None, :], COLS)
    first = np.concatenate([f_re.reshape(-1, tile, rows), f_im.reshape(-1, tile, rows)], axis=1).reshape(2 * rows, rows)
    second = np.block([[s_re, s_im], [-s_im, s_re]])
    back = np.block([[s_re, -s_im], [s_im, s_re]]) / size
    last = np.concatenate([f_re.T, f_im.T])
    twiddle = np.stack([t_re, t_im]).astype(np.float32)
    wide = max(rows, 2 * COLS)
    stacked = np.concatenate([np.pad(t, ((0, 0), (0, wide - t.shape[1]))) for t in (first, last, second, back)])
    return np.stack(halves(stacked)), twiddle


def split(value):
    high = value.astype(BF16)
    return high, (value - high.astype(F32)).astype(BF16)


def dot3(a_hi, a_lo, b_hi, b_lo):
    dot = functools.partial(jnp.dot, preferred_element_type=F32)
    return dot(a_hi, b_hi) + (dot(a_hi, b_lo) + dot(a_lo, b_hi))


def column(row):
    n = row.shape[1]
    eye = lax.broadcasted_iota(jnp.int32, (n, n), 0) == lax.broadcasted_iota(jnp.int32, (n, n), 1)
    return jnp.sum(jnp.where(eye, row, 0.0), axis=1, keepdims=True)


def kernel(
    n, groups, total_channels,
    gate_hbm, key_hbm, value_hbm, filter_hbm, skip_hbm, gain_hbm, *rest,
):
    tables_hbm, (out_hbm, *rest) = rest[:2], rest[2:]
    gate, key, value, filt, skip_ref, gain_ref = rest[:6]
    matrices, twiddle = tables_v = rest[6:8]
    (send_h, send_x, recv_h, recv_x, send_y, recv_y, x_hi, x_lo, mid_hi, mid_lo, spec_h, spec_x, d_hi, d_lo,
     gated, direct, scaled, power, part, parts, mixed,
     load_sems, table_sem, out_sems, in_sems, back_sems, ps_sem, pr_sem, store_sem) = rest[8:]
    rows, wide = spec_h.shape
    tile = min(128, rows)
    f_at, l_at, s_at, b_at = 0, 2 * rows, 4 * rows, 4 * rows + wide
    channels, block = gate.shape
    ctx, ch = lax.axis_index("ctx"), lax.axis_index("ch")
    step = min(16, n)
    ring = min(8, n)
    mesh_id = pl.DeviceIdType.MESH

    def half(ref, slot):
        return ref.at[pl.ds(slot * n, n)]

    pairs = [(half(filter_hbm, 0), half(filt, 0)), (key_hbm, key), (value_hbm, value), (half(filter_hbm, 1), half(filt, 1)),
             (gate_hbm, gate), (skip_hbm, skip_ref), (gain_hbm, gain_ref)]
    loads = [pltpu.make_async_copy(s, d, load_sems.at[i]) for i, (s, d) in enumerate(pairs)]
    table_loads = [pltpu.make_async_copy(s, d, table_sem.at[i]) for i, (s, d) in enumerate(zip(tables_hbm, tables_v))]
    for load in loads[:4]:
        load.start()

    barrier = pltpu.get_barrier_semaphore()

    def hello_ctx(i, _):
        pl.semaphore_signal(barrier, inc=1, device_id={"ctx": lax.rem(ctx + i, n)}, device_id_type=mesh_id)
        return 0

    def hello_ch(i, _):
        pl.semaphore_signal(barrier, inc=1, device_id={"ch": lax.rem(ch + i, groups)}, device_id_type=mesh_id)
        return 0

    lax.fori_loop(1, n, hello_ctx, 0)
    lax.fori_loop(1, groups, hello_ch, 0)

    def peer_of(i):
        j = lax.rem(i, ring)
        odd = lax.rem(j, 2)
        move = odd * ((j + 1) // 2) + (1 - odd) * (ring - j // 2)
        fast = lax.rem(lax.rem(ctx, ring) + move, ring)
        slow = lax.rem(ctx // ring + i // ring, n // ring)
        return slow * ring + fast

    def exchange(src, dst, slot, kind, first=()):
        base = slot * n

        def push(p, group):
            arrival = back_sems.at[slot, group] if kind == 2 else in_sems.at[kind, slot]
            pltpu.make_async_remote_copy(
                src_ref=src.at[base + p], dst_ref=dst.at[base + ctx], send_sem=out_sems.at[kind],
                recv_sem=arrival, device_id={"ctx": p}, device_id_type=mesh_id,
            ).start()

        def one(i, _):
            p = peer_of(i)
            if first:
                later = functools.reduce(jnp.logical_and, [p != q for q in first])
                pl.when(later)(lambda: push(p, i // ring))
            else:
                push(p, i // ring)
            return 0

        for q in first:
            group = lax.rem(q // ring + n // ring - ctx // ring, n // ring)
            pl.when(ctx != q)(lambda q=q, group=group: push(q, group))
        lax.fori_loop(1, n, one, 0)
        dst[pl.ds(base + ctx, 1)] = src[pl.ds(base + ctx, 1)]

    def landed(dst, count, sem):
        some = dst.at[pl.ds(0, count)]
        pltpu.make_async_copy(some, some, sem).wait()

    def lay_filter(slot):
        for c in range(0, n, 8):
            at = pl.ds(slot * n + c, 8)
            send_h[at] = filt[at].reshape(8, block // COLS, COLS)

    def lay_driven(slot):
        for c in range(0, n, step):
            at = pl.ds(slot * n + c, step)
            driven = key[at].astype(F32) * value[at].astype(F32)
            send_x[at] = driven.reshape(step, block // COLS, COLS)

    loads[0].wait()
    pl.semaphore_wait(barrier, (n - 1) + (groups - 1))
    lay_filter(0)
    exchange(send_h, recv_h, 0, 0)
    loads[1].wait()
    loads[2].wait()
    lay_driven(0)
    exchange(send_x, recv_x, 0, 1)
    loads[3].wait()
    lay_filter(1)
    exchange(send_h, recv_h, 1, 0)
    lay_driven(1)
    exchange(send_x, recv_x, 1, 1)
    for load in loads[4:] + table_loads:
        load.start()
    for load in loads[4:]:
        load.wait()

    skip, gain = column(skip_ref[...]), column(gain_ref[...])
    for c in range(0, channels, step):
        at = slice(c, c + step)
        gated[at] = gate[at].astype(F32)
        direct[at] = skip[at] * (key[at].astype(F32) * value[at].astype(F32))
    for load in table_loads:
        load.wait()

    def matrix(start, count, width):
        at = pl.ds(start, count)
        return matrices[0, at, :width], matrices[1, at, :width]

    def forward(src, slot, spec):
        x = src[pl.ds(slot * n, n)].reshape(rows, COLS)
        x_hi[...], x_lo[...] = split(x)

        def first(m, _):
            a = dot3(*matrix(f_at + m * 2 * tile, 2 * tile, rows), x_hi[...], x_lo[...])
            a_re, a_im = a[:tile], a[tile:]
            at = pl.ds(m * tile, tile)
            t_re, t_im = twiddle[0, at], twiddle[1, at]
            mid_hi[at, :COLS], mid_lo[at, :COLS] = split(a_re * t_re - a_im * t_im)
            mid_hi[at, COLS:], mid_lo[at, COLS:] = split(a_re * t_im + a_im * t_re)
            return 0

        def second(m, _):
            at = pl.ds(m * tile, tile)
            spec[at] = dot3(mid_hi[at], mid_lo[at], *matrix(s_at, wide, wide))
            return 0

        lax.fori_loop(0, rows // tile, first, 0)
        lax.fori_loop(0, rows // tile, second, 0)

    def backward(slot):
        def first(m, _):
            at = pl.ds(m * tile, tile)
            x, h = spec_x[at], spec_h[at]
            x_re, x_im, h_re, h_im = x[:, :COLS], x[:, COLS:], h[:, :COLS], h[:, COLS:]
            p = jnp.concatenate([x_re * h_re - x_im * h_im, x_re * h_im + x_im * h_re], axis=1)
            c = dot3(*split(p), *matrix(b_at, wide, wide))
            c_re, c_im = c[:, :COLS], c[:, COLS:]
            t_re, t_im = twiddle[0, at], twiddle[1, at]
            under = pl.ds(rows + m * tile, tile)
            d_hi[at], d_lo[at] = split(c_re * t_re + c_im * t_im)
            d_hi[under], d_lo[under] = split(c_im * t_re - c_re * t_im)
            return 0

        def second(m, _):
            at = pl.ds(m * tile, tile)
            y = dot3(*matrix(l_at + m * tile, tile, rows), d_hi[:rows], d_lo[:rows])
            y += dot3(*matrix(l_at + rows + m * tile, tile, rows), d_hi[rows:], d_lo[rows:])
            blocks = tile // (block // COLS)
            send_y[pl.ds(slot * n + m * blocks, blocks)] = y.reshape(blocks, block // COLS, COLS)
            return 0

        lax.fori_loop(0, rows // tile, first, 0)
        lax.fori_loop(0, rows // tile, second, 0)

    def convolve(slot):
        landed(recv_h, n - 1, in_sems.at[0, slot])
        forward(recv_h, slot, spec_h)
        landed(recv_x, n - 1, in_sems.at[1, slot])
        forward(recv_x, slot, spec_x)
        backward(slot)

    early = tuple(q for q in EARLY if q < n)
    for slot in range(SLOTS):
        convolve(slot)
        exchange(send_y, recv_y, slot, 2, early if slot == SLOTS - 1 else ())

    power[...] = jnp.zeros_like(power)
    for slot in range(SLOTS):
        for away in range(n // ring):
            landed(recv_y, ring - (away == 0), back_sems.at[slot, away])
            owner = lax.rem(ctx // ring + (n // ring - away), n // ring)
            at = pl.ds(pl.multiple_of(slot * n + owner * ring, ring), ring)
            conv = recv_y[at].reshape(ring, block)
            branch = gated[at] * (conv + direct[at])
            scaled[at] = branch
            power[...] += branch * branch
    part[...] = jnp.sum(power[...], axis=0, keepdims=True)

    def share(i, _):
        pltpu.make_async_remote_copy(
            src_ref=part, dst_ref=parts.at[ch], send_sem=ps_sem, recv_sem=pr_sem,
            device_id={"ch": lax.rem(ch + i, groups)}, device_id_type=mesh_id,
        ).start()
        return 0

    lax.fori_loop(1, groups, share, 0)
    parts[pl.ds(ch, 1)] = part[...].reshape(1, 1, block)
    landed(parts, groups - 1, pr_sem)
    mean = jnp.sum(parts[...], axis=0) / total_channels
    norm = lax.rsqrt(mean + 1e-6)
    for c in range(0, channels, step):
        at = slice(c, c + step)
        mixed[at] = (scaled[at] * gain[at] * norm).astype(BF16)
        pltpu.make_async_copy(mixed.at[at], out_hbm.at[at], store_sem).start()

    landed(parts, groups - 1, ps_sem)
    for kind, src in enumerate((send_h, send_x, send_y)):
        landed(src, SLOTS * (n - 1), out_sems.at[kind])
    pltpu.make_async_copy(mixed, out_hbm, store_sem).wait()


def solution(mesh):
    n, groups = mesh.shape["ctx"], mesh.shape["ch"]

    def body(gate_in, key_in, value_in, long_filter, skip_weight, norm_gain):
        channels, block = gate_in.shape
        rows = n * block // COLS
        tile = min(128, rows)
        blocks = pltpu.VMEM((channels, block // COLS, COLS), F32)
        half, full = pltpu.VMEM((channels, block), BF16), pltpu.VMEM((channels, block), F32)
        constants = tables(rows, tile)
        hbm = pl.BlockSpec(memory_space=pltpu.HBM)
        return pl.pallas_call(
            functools.partial(kernel, n, groups, channels * groups),
            out_shape=jax.ShapeDtypeStruct((channels, block), BF16),
            in_specs=[hbm] * (6 + len(constants)),
            out_specs=hbm,
            scratch_shapes=[
                half, half, half, full,
                pltpu.VMEM((1, channels), F32), pltpu.VMEM((1, channels), F32),
                *[pltpu.VMEM(c.shape, c.dtype) for c in constants],
                blocks, blocks, blocks, blocks, blocks, blocks,
                pltpu.VMEM((rows, COLS), BF16), pltpu.VMEM((rows, COLS), BF16),
                pltpu.VMEM((rows, 2 * COLS), BF16), pltpu.VMEM((rows, 2 * COLS), BF16),
                pltpu.VMEM((rows, 2 * COLS), F32), pltpu.VMEM((rows, 2 * COLS), F32),
                pltpu.VMEM((2 * rows, COLS), BF16), pltpu.VMEM((2 * rows, COLS), BF16),
                full, full, full,
                pltpu.VMEM((min(8, n), block), F32),
                pltpu.VMEM((1, block), F32),
                pltpu.VMEM((groups, 1, block), F32),
                half,
                DMA((7,)), DMA((len(constants),)), DMA((3,)), DMA((2, SLOTS)), DMA((SLOTS, n // min(8, n))),
                DMA, DMA, DMA,
            ],
            compiler_params=pltpu.CompilerParams(
                collective_id=0, has_side_effects=True, vmem_limit_bytes=VMEM_LIMIT),
            cost_estimate=pl.CostEstimate(flops=10**10, bytes_accessed=12 * 2**20, transcendentals=4096),
        )(gate_in, key_in, value_in, long_filter, skip_weight.reshape(1, channels), norm_gain.reshape(1, channels),
          *[jnp.asarray(c) for c in constants])

    specs = (P("ch", "ctx"), P("ch", "ctx"), P("ch", "ctx"), P("ch", "ctx"), P("ch"), P("ch"))
    return jax.shard_map(body, mesh=mesh, in_specs=specs, out_specs=P("ch", "ctx"), check_vma=False)
```

```python
import functools

import jax
import jax.numpy as jnp
import ml_dtypes
import numpy as np
from jax import lax
from jax.experimental import pallas as pl
from jax.experimental.pallas import tpu as pltpu
from jax.sharding import PartitionSpec as P

COLS = 256
SLOTS = 2
F32, BF16 = jnp.float32, jnp.bfloat16
VMEM_LIMIT = 53 * 2**20
EARLY = (0, 24, 8, 1, 16, 25, 9, 2, 17, 10, 26, 18, 3, 11, 27, 19)
DMA = pltpu.SemaphoreType.DMA


def turn(num, den):
    angle = 2.0 * np.pi * ((num % den) / den)
    return np.cos(angle), -np.sin(angle)


def halves(table):
    table = table.astype(np.float32)
    high = table.astype(ml_dtypes.bfloat16)
    low = (table - high.astype(np.float32)).astype(ml_dtypes.bfloat16)
    return high, low


def tables(rows, tile):
    size = rows * COLS
    freq = 4 * np.arange(rows, dtype=np.int64) + 1
    row, col = np.arange(rows, dtype=np.int64), np.arange(COLS, dtype=np.int64)
    f_re, f_im = turn(freq[:, None] * row[None, :], 4 * rows)
    t_re, t_im = turn(freq[:, None] * col[None, :], 4 * size)
    s_re, s_im = turn(col[:, None] * col[None, :], COLS)
    first = np.concatenate([f_re.reshape(-1, tile, rows), f_im.reshape(-1, tile, rows)], axis=1).reshape(2 * rows, rows)
    second = np.block([[s_re, s_im], [-s_im, s_re]])
    back = np.block([[s_re, -s_im], [s_im, s_re]]) / size
    last = np.concatenate([f_re.T, f_im.T])
    twiddle = np.stack([t_re, t_im]).astype(np.float32)
    wide = max(rows, 2 * COLS)
    stacked = np.concatenate([np.pad(t, ((0, 0), (0, wide - t.shape[1]))) for t in (first, last, second, back)])
    return np.stack(halves(stacked)), twiddle


def split(value):
    high = value.astype(BF16)
    return high, (value - high.astype(F32)).astype(BF16)


def dot3(a_hi, a_lo, b_hi, b_lo):
    dot = functools.partial(jnp.dot, preferred_element_type=F32)
    return dot(a_hi, b_hi) + (dot(a_hi, b_lo) + dot(a_lo, b_hi))


def column(row):
    n = row.shape[1]
    eye = lax.broadcasted_iota(jnp.int32, (n, n), 0) == lax.broadcasted_iota(jnp.int32, (n, n), 1)
    return jnp.sum(jnp.where(eye, row, 0.0), axis=1, keepdims=True)


def kernel(
    n, groups, total_channels,
    gate_hbm, key_hbm, value_hbm, filter_hbm, weights_hbm, *rest,
):
    tables_hbm, (out_hbm, *rest) = rest[:2], rest[2:]
    gate, key, value, filt, weights = rest[:5]
    matrices, twiddle = tables_v = rest[5:7]
    (send_h, send_x, recv_h, recv_x, send_y, recv_y, x_hi, x_lo, mid_hi, mid_lo, spec_h, spec_x, d_hi, d_lo,
     gated, direct, scaled, power, part, parts, mixed,
     load_sems, table_sem, out_sems, in_sems, back_sems, ps_sem, pr_sem, store_sem) = rest[7:]
    rows, wide = spec_h.shape
    tile = min(128, rows)
    f_at, l_at, s_at, b_at = 0, 2 * rows, 4 * rows, 4 * rows + wide
    channels, block = gate.shape
    ctx, ch = lax.axis_index("ctx"), lax.axis_index("ch")
    step = min(16, n)
    ring = min(8, n)
    mesh_id = pl.DeviceIdType.MESH

    def half(ref, slot):
        return ref.at[pl.ds(slot * n, n)]

    pairs = [(half(filter_hbm, 0), half(filt, 0)), (key_hbm, key), (value_hbm, value), (half(filter_hbm, 1), half(filt, 1)),
             (gate_hbm, gate), (weights_hbm, weights)]
    loads = [pltpu.make_async_copy(s, d, load_sems.at[i]) for i, (s, d) in enumerate(pairs)]
    table_loads = [pltpu.make_async_copy(s, d, table_sem.at[i]) for i, (s, d) in enumerate(zip(tables_hbm, tables_v))]
    for load in loads[:4]:
        load.start()

    barrier = pltpu.get_barrier_semaphore()

    def hello_ctx(i, _):
        pl.semaphore_signal(barrier, inc=1, device_id={"ctx": lax.rem(ctx + i, n)}, device_id_type=mesh_id)
        return 0

    def hello_ch(i, _):
        pl.semaphore_signal(barrier, inc=1, device_id={"ch": lax.rem(ch + i, groups)}, device_id_type=mesh_id)
        return 0

    lax.fori_loop(1, n, hello_ctx, 0)
    lax.fori_loop(1, groups, hello_ch, 0)

    def peer_of(i):
        j = lax.rem(i, ring)
        odd = lax.rem(j, 2)
        move = odd * ((j + 1) // 2) + (1 - odd) * (ring - j // 2)
        fast = lax.rem(lax.rem(ctx, ring) + move, ring)
        slow = lax.rem(ctx // ring + i // ring, n // ring)
        return slow * ring + fast

    def exchange(src, dst, slot, kind, first=()):
        base = slot * n

        def push(p, group):
            arrival = back_sems.at[slot, group] if kind == 2 else in_sems.at[kind, slot]
            pltpu.make_async_remote_copy(
                src_ref=src.at[base + p], dst_ref=dst.at[base + ctx], send_sem=out_sems.at[kind],
                recv_sem=arrival, device_id={"ctx": p}, device_id_type=mesh_id,
            ).start()

        def one(step, _):
            i = n - step
            p = peer_of(i)
            if first:
                later = functools.reduce(jnp.logical_and, [p != q for q in first])
                pl.when(later)(lambda: push(p, i // ring))
            else:
                push(p, i // ring)
            return 0

        for q in first:
            group = lax.rem(q // ring + n // ring - ctx // ring, n // ring)
            pl.when(ctx != q)(lambda q=q, group=group: push(q, group))
        lax.fori_loop(1, n, one, 0)
        dst[pl.ds(base + ctx, 1)] = src[pl.ds(base + ctx, 1)]

    def landed(dst, count, sem):
        some = dst.at[pl.ds(0, count)]
        pltpu.make_async_copy(some, some, sem).wait()

    def lay_filter(slot):
        for c in range(0, n, 8):
            at = pl.ds(slot * n + c, 8)
            send_h[at] = filt[at].reshape(8, block // COLS, COLS)

    def lay_driven(slot):
        for c in range(0, n, step):
            at = pl.ds(slot * n + c, step)
            driven = key[at].astype(F32) * value[at].astype(F32)
            send_x[at] = driven.reshape(step, block // COLS, COLS)

    loads[0].wait()
    pl.semaphore_wait(barrier, (n - 1) + (groups - 1))
    lay_filter(0)
    exchange(send_h, recv_h, 0, 0)
    loads[1].wait()
    loads[2].wait()
    lay_driven(0)
    exchange(send_x, recv_x, 0, 1)
    loads[3].wait()
    lay_filter(1)
    exchange(send_h, recv_h, 1, 0)
    lay_driven(1)
    exchange(send_x, recv_x, 1, 1)
    for load in loads[4:] + table_loads:
        load.start()
    for load in loads[4:]:
        load.wait()

    both = column(weights[...])
    skip, gain = both[:channels], both[channels:]
    for c in range(0, channels, step):
        at = slice(c, c + step)
        gated[at] = gate[at].astype(F32)
        direct[at] = skip[at] * (key[at].astype(F32) * value[at].astype(F32))
    for load in table_loads:
        load.wait()

    def matrix(start, count, width):
        at = pl.ds(start, count)
        return matrices[0, at, :width], matrices[1, at, :width]

    def forward(src, slot, spec):
        x = src[pl.ds(slot * n, n)].reshape(rows, COLS)
        x_hi[...], x_lo[...] = split(x)

        def first(m, _):
            a = dot3(*matrix(f_at + m * 2 * tile, 2 * tile, rows), x_hi[...], x_lo[...])
            a_re, a_im = a[:tile], a[tile:]
            at = pl.ds(m * tile, tile)
            t_re, t_im = twiddle[0, at], twiddle[1, at]
            mid_hi[at, :COLS], mid_lo[at, :COLS] = split(a_re * t_re - a_im * t_im)
            mid_hi[at, COLS:], mid_lo[at, COLS:] = split(a_re * t_im + a_im * t_re)
            return 0

        def second(m, _):
            at = pl.ds(m * tile, tile)
            spec[at] = dot3(mid_hi[at], mid_lo[at], *matrix(s_at, wide, wide))
            return 0

        lax.fori_loop(0, rows // tile, first, 0)
        lax.fori_loop(0, rows // tile, second, 0)

    def backward(slot):
        def first(m, _):
            at = pl.ds(m * tile, tile)
            x, h = spec_x[at], spec_h[at]
            x_re, x_im, h_re, h_im = x[:, :COLS], x[:, COLS:], h[:, :COLS], h[:, COLS:]
            p = jnp.concatenate([x_re * h_re - x_im * h_im, x_re * h_im + x_im * h_re], axis=1)
            c = dot3(*split(p), *matrix(b_at, wide, wide))
            c_re, c_im = c[:, :COLS], c[:, COLS:]
            t_re, t_im = twiddle[0, at], twiddle[1, at]
            under = pl.ds(rows + m * tile, tile)
            d_hi[at], d_lo[at] = split(c_re * t_re + c_im * t_im)
            d_hi[under], d_lo[under] = split(c_im * t_re - c_re * t_im)
            return 0

        def second(m, _):
            at = pl.ds(m * tile, tile)
            y = dot3(*matrix(l_at + m * tile, tile, rows), d_hi[:rows], d_lo[:rows])
            y += dot3(*matrix(l_at + rows + m * tile, tile, rows), d_hi[rows:], d_lo[rows:])
            blocks = tile // (block // COLS)
            send_y[pl.ds(slot * n + m * blocks, blocks)] = y.reshape(blocks, block // COLS, COLS)
            return 0

        lax.fori_loop(0, rows // tile, first, 0)
        lax.fori_loop(0, rows // tile, second, 0)

    def convolve(slot):
        landed(recv_h, n - 1, in_sems.at[0, slot])
        forward(recv_h, slot, spec_h)
        landed(recv_x, n - 1, in_sems.at[1, slot])
        forward(recv_x, slot, spec_x)
        backward(slot)

    early = tuple(q for q in EARLY if q < n)
    for slot in range(SLOTS):
        convolve(slot)
        exchange(send_y, recv_y, slot, 2, early if slot == SLOTS - 1 else ())

    power[...] = jnp.zeros_like(power)
    for slot in range(SLOTS):
        for away in range(n // ring):
            landed(recv_y, ring - (away == 0), back_sems.at[slot, away])
            owner = lax.rem(ctx // ring + (n // ring - away), n // ring)
            at = pl.ds(pl.multiple_of(slot * n + owner * ring, ring), ring)
            conv = recv_y[at].reshape(ring, block)
            branch = gated[at] * (conv + direct[at])
            scaled[at] = branch
            power[...] += branch * branch
    part[...] = jnp.sum(power[...], axis=0, keepdims=True)

    def share(i, _):
        pltpu.make_async_remote_copy(
            src_ref=part, dst_ref=parts.at[ch], send_sem=ps_sem, recv_sem=pr_sem,
            device_id={"ch": lax.rem(ch + i, groups)}, device_id_type=mesh_id,
        ).start()
        return 0

    lax.fori_loop(1, groups, share, 0)
    parts[pl.ds(ch, 1)] = part[...].reshape(1, 1, block)
    landed(parts, groups - 1, pr_sem)
    mean = jnp.sum(parts[...], axis=0) / total_channels
    norm = lax.rsqrt(mean + 1e-6)
    for c in range(0, channels, step):
        at = slice(c, c + step)
        mixed[at] = (scaled[at] * gain[at] * norm).astype(BF16)
        pltpu.make_async_copy(mixed.at[at], out_hbm.at[at], store_sem).start()

    landed(parts, groups - 1, ps_sem)
    for kind, src in enumerate((send_h, send_x, send_y)):
        landed(src, SLOTS * (n - 1), out_sems.at[kind])
    pltpu.make_async_copy(mixed, out_hbm, store_sem).wait()


def solution(mesh):
    n, groups = mesh.shape["ctx"], mesh.shape["ch"]

    def body(gate_in, key_in, value_in, long_filter, skip_weight, norm_gain):
        channels, block = gate_in.shape
        rows = n * block // COLS
        tile = min(128, rows)
        blocks = pltpu.VMEM((channels, block // COLS, COLS), F32)
        half, full = pltpu.VMEM((channels, block), BF16), pltpu.VMEM((channels, block), F32)
        constants = tables(rows, tile)
        hbm = pl.BlockSpec(memory_space=pltpu.HBM)
        return pl.pallas_call(
            functools.partial(kernel, n, groups, channels * groups),
            out_shape=jax.ShapeDtypeStruct((channels, block), BF16),
            in_specs=[hbm] * (5 + len(constants)),
            out_specs=pl.BlockSpec(memory_space=pltpu.VMEM),
            scratch_shapes=[
                half, half, half, full,
                pltpu.VMEM((1, 2 * channels), F32),
                *[pltpu.VMEM(c.shape, c.dtype) for c in constants],
                blocks, blocks, blocks, blocks, blocks, blocks,
                pltpu.VMEM((rows, COLS), BF16), pltpu.VMEM((rows, COLS), BF16),
                pltpu.VMEM((rows, 2 * COLS), BF16), pltpu.VMEM((rows, 2 * COLS), BF16),
                pltpu.VMEM((rows, 2 * COLS), F32), pltpu.VMEM((rows, 2 * COLS), F32),
                pltpu.VMEM((2 * rows, COLS), BF16), pltpu.VMEM((2 * rows, COLS), BF16),
                full, full, full,
                pltpu.VMEM((min(8, n), block), F32),
                pltpu.VMEM((1, block), F32),
                pltpu.VMEM((groups, 1, block), F32),
                half,
                DMA((6,)), DMA((len(constants),)), DMA((3,)), DMA((2, SLOTS)), DMA((SLOTS, n // min(8, n))),
                DMA, DMA, DMA,
            ],
            compiler_params=pltpu.CompilerParams(
                collective_id=0, has_side_effects=True, vmem_limit_bytes=VMEM_LIMIT),
            cost_estimate=pl.CostEstimate(flops=10**10, bytes_accessed=12 * 2**20, transcendentals=4096),
        )(gate_in, key_in, value_in, long_filter, jnp.concatenate([skip_weight, norm_gain]).reshape(1, 2 * channels),
          *[jnp.asarray(c) for c in constants])

    specs = (P("ch", "ctx"), P("ch", "ctx"), P("ch", "ctx"), P("ch", "ctx"), P("ch"), P("ch"))
    return jax.shard_map(body, mesh=mesh, in_specs=specs, out_specs=P("ch", "ctx"), check_vma=False)
```
